256 devices in a mesh: ri: 8 (over y, core), mu: 4 (over x), nu: 8 (over z).
Axes of the slice: x: 4, y: 4, z: 8, core: 2. Of those that a mesh axis runs over, the one named last changes fastest.
Arguments:
- three_center: bfloat16 [32, 2304, 128, 128], P('ri', ('mu', 'nu')), may hold values from -0.15625 to 0.15625
- block_pairs: int32 [2304, 2], P(('mu', 'nu')), may hold values from -1 to 95, as said below
- occ_factor: bfloat16 [12288, 128], P(('mu', 'nu')), may hold values from -6 to 6
- virt_density: bfloat16 [12288, 12288], P(('mu', 'nu'), 'ri'), may hold values from -0.0546875 to 0.0546875
- block_sizes: int32 [96], replicated, may hold values from 96 to 128
- occ_mask: int32 [96], replicated, may hold values 0 or 1
- virt_mask: int32 [96, 96], replicated, may hold values 0 or 1
Outputs:
- transformed: bfloat16 [32, 12288, 128], P('ri', ('mu', 'nu'))
The draws below stay inside these ranges and needn't reach their ends.
Inputs may be any that keep to these rules, and one draw needn't show every extreme that they name: `block_pairs`: slots k in [d * 72, (d + 1) * 72) belong to device d of mu+nu; a live slot holds a mu block of that device's mu range (the range of 24 blocks of its mu index) and any nu block; empty slots hold -1 in both columns, and the live slots of a device come first. Every mu block appears in exactly 12 live slots, with distinct nu blocks. A device holds at most 72 live slots, and in every mu range some device holds exactly 72.
All inputs are finite; a program needn't handle non-finite values.
Results may differ from the reference program's by a relative error of at most 0.015.
Values may be sent and summed in bfloat16 or wider, within the bound.
A program may use at most 128 MiB of HBM per device.

```python
import jax
import jax.numpy as jnp
from jax import lax

BS = 128
NB = 96
KB = 12
OCC = 128
N = 12288
RI = 32
GRID_MU = 4
GRID_NU = 8
ROWPAIRS = 288
CAP = 72
PAIRS = 2304


def draw_block_pairs(key, part):
    keys = jax.random.split(key, 4)
    band = NB
    band_scores = jax.random.randint(keys[0], (NB, band), 0, 1 << 20) * band + jnp.arange(band, dtype=jnp.int32)[None, :]
    picked = jnp.argsort(band_scores, axis=1)[:, :KB].astype(jnp.int32)
    offsets = picked - band // 2
    nu_blocks = (jnp.arange(NB, dtype=jnp.int32)[:, None] + offsets) % NB
    mu_blocks = jnp.broadcast_to(jnp.arange(NB, dtype=jnp.int32)[:, None], (NB, KB))
    mu_rows = mu_blocks.reshape(GRID_MU, ROWPAIRS)
    nu_rows = nu_blocks.reshape(GRID_MU, ROWPAIRS)
    pair_scores = jax.random.randint(keys[1], (GRID_MU, ROWPAIRS), 0, 1 << 20) * ROWPAIRS + jnp.arange(ROWPAIRS, dtype=jnp.int32)[None, :]
    shuffle = jnp.argsort(pair_scores, axis=1).astype(jnp.int32)
    mu_rows = jnp.take_along_axis(mu_rows, shuffle, axis=1)
    nu_rows = jnp.take_along_axis(nu_rows, shuffle, axis=1)
    others = GRID_NU - 1
    rest = ROWPAIRS - CAP
    base = rest // others
    remain = rest % others
    other_index = jnp.arange(others, dtype=jnp.int32)
    counts_other = base + (other_index < remain).astype(jnp.int32)
    halves = others // 2
    shifts = jax.random.randint(keys[2], (GRID_MU, halves), 0, base // 2 + 1)
    delta = jnp.zeros((GRID_MU, others), jnp.int32)
    delta = delta.at[:, 0:2 * halves:2].add(shifts)
    delta = delta.at[:, 1:2 * halves:2].add(-shifts)
    counts_other = counts_other[None, :] + delta
    special = jax.random.randint(keys[3], (GRID_MU,), 0, GRID_NU)
    position = jnp.arange(GRID_NU, dtype=jnp.int32)[None, :]
    source = jnp.clip(position - (position > special[:, None]).astype(jnp.int32), 0, others - 1)
    counts = jnp.where(position == special[:, None], CAP, jnp.take_along_axis(counts_other, source, axis=1))
    starts = jnp.cumsum(counts, axis=1) - counts
    slot_index = jnp.arange(CAP, dtype=jnp.int32)
    slot_live = slot_index[None, None, :] < counts[:, :, None]
    where_index = jnp.clip(starts[:, :, None] + slot_index[None, None, :], 0, ROWPAIRS - 1).reshape(GRID_MU, GRID_NU * CAP)
    mu_pick = jnp.take_along_axis(mu_rows, where_index, axis=1).reshape(GRID_MU, GRID_NU, CAP)
    nu_pick = jnp.take_along_axis(nu_rows, where_index, axis=1).reshape(GRID_MU, GRID_NU, CAP)
    mu_out = jnp.where(slot_live, mu_pick, -1)
    nu_out = jnp.where(slot_live, nu_pick, -1)
    return jnp.stack([mu_out, nu_out], axis=-1).reshape(PAIRS, 2).astype(jnp.int32)


def set_ends(entries, stream_key, low, top_value):
    longest = entries.shape.index(max(entries.shape))
    spots = []
    for shift in (0, 1):
        where = [jax.random.randint(jax.random.fold_in(stream_key, axis), (), 0, length) for axis, length in enumerate(entries.shape)]
        where[longest] = (where[longest] + shift) % entries.shape[longest]
        spots.append(tuple(where))
    return entries.at[spots[0]].set(low).at[spots[1]].set(top_value)


def block_scale(rng, shape, pieces, smallest, high):
    factor_of = 1.0
    for dim, blocks in pieces:
        steps = jax.random.uniform(jax.random.fold_in(jax.random.fold_in(rng, 6), dim), (blocks,), jnp.float32, smallest / len(pieces), high / len(pieces))
        factor_of = factor_of * jnp.repeat(jnp.exp(steps), shape[dim] // blocks).reshape((-1,) + (1,) * (len(shape) - 1 - dim))
    return factor_of


def scatter_about(own_key, shape, width, most, cuts=(), kind=jnp.bfloat16):
    loudness = block_scale(own_key, shape, cuts, -0.22, 0.18) if cuts else 1.0
    values = jax.random.normal(own_key, shape, jnp.float32) * width * loudness
    return jnp.minimum(jnp.maximum(values, -most), most).astype(kind)


def setup_inputs(seed: int = 0) -> dict:
    streams_of = jax.random.split(jax.random.key(seed), 8)
    three_center = scatter_about(streams_of[0], (RI, PAIRS, BS, BS), (KB * BS) ** -0.5, 0.15625, ((0, 8), (1, 32)))
    block_pairs = draw_block_pairs(jax.random.fold_in(streams_of[7], 71), 0)
    occ_factor = scatter_about(streams_of[2], (N, OCC), 1.0, 6.0, ((0, 32),))
    virt_density = scatter_about(streams_of[3], (N, N), N ** -0.5, 0.0546875, ((0, 32), (1, 8)))
    block_sizes = set_ends(jax.random.randint(streams_of[4], (NB,), BS * 3 // 4, BS + 1), jax.random.fold_in(streams_of[4], 1), BS * 3 // 4, BS).astype(jnp.int32)
    occ_mask = set_ends((jax.random.randint(streams_of[5], (NB,), 0, 4) < 3).astype(jnp.int32), jax.random.fold_in(streams_of[5], 1), 0, 1)
    virt_mask = set_ends((jax.random.randint(streams_of[6], (NB, NB), 0, 4) < 3).astype(jnp.int32), jax.random.fold_in(streams_of[6], 1), 0, 1)
    return {"three_center": three_center, "block_pairs": block_pairs, "occ_factor": occ_factor, "virt_density": virt_density, "block_sizes": block_sizes, "occ_mask": occ_mask, "virt_mask": virt_mask}


def reference(three_center, block_pairs, occ_factor, virt_density, block_sizes, occ_mask, virt_mask):
    total_rows = NB * BS
    inside = jnp.arange(BS, dtype=jnp.int32)[None, :] < block_sizes[:, None]
    keep_occ = (inside & (occ_mask[:, None] > 0)).reshape(total_rows)
    occ_kept = jnp.where(keep_occ[:, None], occ_factor, jnp.zeros((), occ_factor.dtype))
    keep_virt = (virt_mask[:, None, :, None] > 0) & inside[:, :, None, None] & inside[None, None, :, :]
    virt_kept = jnp.where(keep_virt, virt_density.reshape(NB, BS, NB, BS), jnp.zeros((), virt_density.dtype))
    virt_kept = virt_kept.reshape(total_rows, total_rows)
    slot_live = (block_pairs[:, 0] >= 0).astype(jnp.float32)
    mu_block = jnp.clip(block_pairs[:, 0], 0, NB - 1).astype(jnp.int32)
    nu_block = jnp.clip(block_pairs[:, 1], 0, NB - 1).astype(jnp.int32)
    occ_blocks = occ_kept.reshape(NB, BS, OCC)[nu_block].astype(jnp.float32)

    def half_transform(ri_slab):
        products = jnp.einsum("kab,kbo->kao", ri_slab.astype(jnp.float32), occ_blocks)
        products = products * slot_live[:, None, None]
        summed = jax.ops.segment_sum(products, mu_block, num_segments=NB)
        return summed.reshape(total_rows, OCC).astype(jnp.bfloat16)

    half_rows = lax.map(half_transform, three_center)

    def full_transform(slab_rows):
        return jnp.dot(virt_kept, slab_rows, preferred_element_type=jnp.float32).astype(jnp.bfloat16)

    return lax.map(full_transform, half_rows)
```

```python
import functools

import jax
import jax.numpy as jnp
from jax import lax
from jax.experimental import pallas as pl
from jax.experimental.pallas import tpu as pltpu
from jax.sharding import PartitionSpec as P

MESH = pl.DeviceIdType.MESH
BS = 128
STAGGER = 2
SLOTS_A_STEP = 8
MIB = 1 << 20


class Copies:
    def __init__(self, send, recv):
        self.send, self.recv, self.used = send, recv, 0
        self.started = []

    def make(self, src, dst, device):
        i = self.used
        self.used += 1
        return pltpu.make_async_remote_copy(
            src_ref=src,
            dst_ref=dst,
            send_sem=self.send.at[i],
            recv_sem=self.recv.at[i],
            device_id=device,
            device_id_type=MESH,
        )

    def go(self, src, dst, device):
        copy = self.make(src, dst, device)
        copy.start()
        self.started.append(copy)
        return copy

    def wait_sends(self):
        for copy in self.started:
            copy.wait_send()


def greet(devices):
    barrier = pltpu.get_barrier_semaphore()
    for device in devices:
        pl.semaphore_signal(barrier, inc=1, device_id=device, device_id_type=MESH)
    pl.semaphore_wait(barrier, len(devices))


def occ_copies(x_size, z_size):
    return 4 * (z_size // 2) // 2 + 4 * z_size + x_size


def gather_occ(cores, x_size, z_size, occ_ref, all_ref, send, recv):
    x, z, r = lax.axis_index("mu"), lax.axis_index("nu"), lax.axis_index("ri")
    c = lax.rem(r, cores)
    zp, zm = {"nu": lax.rem(z + 1, z_size)}, {"nu": lax.rem(z + z_size - 1, z_size)}
    x_up, x_down = lax.rem(x + 1, x_size), lax.rem(x + x_size - 1, x_size)
    x_far = lax.rem(x + 2, x_size)
    xp, xm = {"mu": x_up}, {"mu": x_down}
    sibling = {"ri": r + 1 - 2 * c}
    rows = occ_ref.shape[0] // cores
    mine = pl.ds(pl.multiple_of(c * rows, 16), rows)
    first = pl.ds(pl.multiple_of(c * rows, 16), rows // 2)
    second = pl.ds(pl.multiple_of(c * rows + rows // 2, 16), rows // 2)
    far = z_size // 2
    greet([zp, zm, xp, xm, sibling])
    copies = Copies(send, recv)

    def here(column, shard, part):
        return all_ref.at[column, shard, part]

    def along_x(shard):
        ref = here(x, shard, mine)
        return shard, copies.go(ref, ref, xp), copies.go(ref, ref, xm)

    def pass_on(sent):
        shard, up, down = sent
        up.wait_recv()
        ref = here(x_down, shard, first)
        one = copies.go(ref, ref, xp)
        down.wait_recv()
        ref = here(x_up, shard, second)
        return one, copies.go(ref, ref, xm)

    all_ref[x, z, mine, :] = occ_ref[mine, :]
    ups, downs, waiting, passed = [], [], [], []
    for t in range(far):
        behind, ahead = lax.rem(z + z_size - t, z_size), lax.rem(z + t, z_size)
        last = t == far - 1
        if t:
            ups[-1].wait_recv()
        ref = here(x, behind, first if last else mine)
        ups.append(copies.go(ref, ref, zp))
        if t:
            downs[-1].wait_recv()
        ref = here(x, ahead, second if last else mine)
        downs.append(copies.go(ref, ref, zm))
        new = [along_x(behind)]
        if t:
            new.append(along_x(ahead))
        for sent in waiting:
            passed.append(pass_on(sent))
        waiting = new
    ups[-1].wait_recv()
    downs[-1].wait_recv()
    waiting.append(along_x(lax.rem(z + far, z_size)))
    over = [copies.go(all_ref.at[x, :, mine], all_ref.at[x, :, mine], sibling)]
    for sent in waiting:
        passed.append(pass_on(sent))
    for column in (x_down, x_up):
        ref = all_ref.at[column, :, mine]
        over.append(copies.go(ref, ref, sibling))
    for one, two in passed:
        one.wait_recv()
        two.wait_recv()
    ref = all_ref.at[x_far, :, mine]
    over.append(copies.go(ref, ref, sibling))
    for copy in over:
        copy.wait_recv()
    copies.wait_sends()


def half_transform(
    pairs, sizes, occ_mask, virt_mask, three_ref, occ_ref, virt_ref, part_ref, kept_ref, total
):
    g = pl.program_id(0)
    p_rows, slots = three_ref.shape[0], three_ref.shape[1]
    blocks = total.shape[1]
    occ_cols = occ_ref.shape[-1]
    first_block = lax.axis_index("mu") * blocks
    row_blocks, col_blocks = virt_ref.shape[0] // BS, virt_ref.shape[1] // BS
    row_ids = lax.broadcasted_iota(jnp.int32, (BS, BS), 0)
    col_ids = lax.broadcasted_iota(jnp.int32, (BS, BS), 1)
    occ_rows = lax.broadcasted_iota(jnp.int32, (BS, occ_cols), 0)

    @pl.when(g == 0)
    def _():
        total[...] = jnp.zeros_like(total)

    for j in range(slots):
        k = g * slots + j
        mu, nu = pairs[k, 0], pairs[k, 1]

        @pl.when(mu >= 0)
        def _(j=j, mu=mu, nu=nu):
            kept_rows = jnp.where(occ_mask[nu] > 0, sizes[nu], 0)
            occ = jnp.where(occ_rows < kept_rows, occ_ref[nu].astype(jnp.float32), 0.0)
            product = jnp.dot(
                three_ref[:, j].reshape(p_rows * BS, BS),
                occ.astype(jnp.bfloat16),
                preferred_element_type=jnp.float32,
            )
            total[:, mu - first_block] += product.reshape(p_rows, BS, occ_cols)

    @pl.when(g < row_blocks)
    def _():
        s_block = (lax.axis_index("mu") * lax.axis_size("nu") + lax.axis_index("nu")) * row_blocks + g
        rows = pl.ds(pl.multiple_of(g * BS, BS), BS)
        for b in range(col_blocks):
            m_block = lax.axis_index("ri") * col_blocks + b
            cols = pl.ds(b * BS, BS)
            kept_rows = jnp.where(virt_mask[s_block, m_block] > 0, sizes[s_block], 0)
            keep = (row_ids < kept_rows) & (col_ids < sizes[m_block])
            kept = jnp.where(keep, virt_ref[rows, cols].astype(jnp.float32), 0.0)
            kept_ref[rows, cols] = kept.astype(jnp.bfloat16)

    @pl.when(g == pl.num_programs(0) - 1)
    def _():
        part_ref[...] = total[...].astype(jnp.bfloat16)


def exchange_copies(x_size, z_size):
    return x_size * (4 * (z_size // 2)) + x_size + 6 + x_size


def exchange(
    cores, x_size, z_size,
    part_ref, virt_ref, out_ref,
    tile, sums, reduced, half, partial, landed,
    send, recv, plane_send, plane_recv, out_send, out_recv, own_sem,
):
    x, z, r = lax.axis_index("mu"), lax.axis_index("nu"), lax.axis_index("ri")
    c, y = lax.rem(r, cores), r // cores
    y_size = x_size
    far = z_size // 2
    rows, occ_cols = part_ref.shape[2], part_ref.shape[3]
    zp, zm = {"nu": lax.rem(z + 1, z_size)}, {"nu": lax.rem(z + z_size - 1, z_size)}
    x_up, x_down = lax.rem(x + 1, x_size), lax.rem(x + x_size - 1, x_size)
    x_far = lax.rem(x + 2, x_size)
    xp, xm = {"mu": x_up}, {"mu": x_down}
    sibling = {"ri": r + 1 - 2 * c}
    first, second = pl.ds(0, rows // 2), pl.ds(rows // 2, rows // 2)
    sides = (first, second)
    plane = [
        {"ri": lax.rem(y + b, y_size) * cores + c, "mu": lax.rem(x + a, x_size)}
        for b in range(y_size)
        for a in range(x_size)
        if a or b
    ]
    greet([zp, zm, sibling] + plane)
    copies = Copies(send, recv)
    ahead = lambda t: lax.rem(z + t + z_size, z_size)
    towards = (zp, zm)
    chunks = range(x_size)
    which = [lax.rem(k - y + y_size, y_size) for k in chunks]
    itself = [(x == y) & (which[k] == x) for k in chunks]
    scattering = {}
    moving = {}
    gathering = {}
    leaving = []

    def scatter(t, k):
        for d in (0, 1):
            shard = ahead(far - t if d == 0 else t - far)
            if t == 0:
                src = part_ref.at[which[k], shard, sides[d]]
                dst = sums.at[d, k, 0, sides[d]]
            else:
                scattering[d, k, t - 1].wait_recv()
                src = sums.at[d, k, t - 1]
                dst = sums.at[d, k, t]
                if t == 1:
                    a, b = sides[d], sides[1 - d]
                    added = src[a, :].astype(jnp.float32) + part_ref[which[k], shard, a, :].astype(jnp.float32)
                    src[a, :] = added.astype(jnp.bfloat16)
                    src[b, :] = part_ref[which[k], shard, b, :]
                else:
                    added = src[...].astype(jnp.float32) + part_ref[which[k], shard].astype(jnp.float32)
                    src[...] = added.astype(jnp.bfloat16)
            scattering[d, k, t] = copies.go(src, dst, towards[d])

    def move(k):
        for d in (0, 1):
            scattering[d, k, far - 1].wait_recv()
        added = part_ref[which[k], z].astype(jnp.float32)
        added += sums[0, k, far - 1].astype(jnp.float32) + sums[1, k, far - 1].astype(jnp.float32)
        added = added.astype(jnp.bfloat16)
        copy = moving[k] = pltpu.make_async_remote_copy(
            src_ref=reduced.at[k],
            dst_ref=half.at[k, z],
            send_sem=plane_send.at[k],
            recv_sem=plane_recv.at[k],
            device_id={"ri": x * cores + c, "mu": which[k]},
            device_id_type=MESH,
        )

        @pl.when(itself[k])
        def _():
            half[k, z] = added

        @pl.when(jnp.logical_not(itself[k]))
        def _():
            reduced[k] = added
            copy.start()

    def gather(t, k):
        if t == 0:

            @pl.when(jnp.logical_not(itself[k]))
            def _():
                moving[k].wait_recv()

        for d in (0, 1):
            if t:
                gathering[d, k, t - 1].wait_recv()
            shard = ahead(-t if d == 0 else t)
            ref = half.at[k, shard, sides[d]] if t == far - 1 else half.at[k, shard]
            gathering[d, k, t] = copies.go(ref, ref, towards[d])

    def gathered(k):
        for d in (0, 1):
            gathering[d, k, far - 1].wait_recv()

    depth = z_size // cores
    width = depth * rows

    def product(k, turn):
        off = (2, 1, 3, 0)[turn]
        column = lax.rem(x + off, x_size)
        value = None
        for b in range(cores):
            shards = half[k, b * depth : (b + 1) * depth].reshape(width, occ_cols)
            term = jnp.dot(tile[column, b], shards, preferred_element_type=jnp.float32)
            value = term if value is None else value + term
        value = value.astype(jnp.bfloat16)
        to_y = lax.rem(k - x + y_size, y_size)
        copy = pltpu.make_async_remote_copy(
            src_ref=partial.at[k, off],
            dst_ref=landed.at[x, y],
            send_sem=out_send.at[k * x_size + off],
            recv_sem=out_recv.at[x * y_size + y],
            device_id={"ri": to_y * cores + c, "mu": column},
            device_id_type=MESH,
        )
        if off:
            partial[k, off] = value
            copy.start()
            leaving.append((None, copy))
            return
        remote = to_y != y

        @pl.when(remote)
        def _():
            partial[k, off] = value
            copy.start()

        @pl.when(jnp.logical_not(remote))
        def _():
            landed[x, y] = value

        leaving.append((remote, copy))

    def finish(k):
        i = which[k]
        for b in range(y_size):
            arrival = pltpu.make_async_remote_copy(
                src_ref=partial.at[k, 0],
                dst_ref=landed.at[i, b],
                send_sem=out_send.at[k * x_size],
                recv_sem=out_recv.at[i * y_size + b],
                device_id=zp,
                device_id_type=MESH,
            )

            @pl.when(jnp.logical_not((i == x) & (y == b)))
            def _(arrival=arrival):
                arrival.wait_recv()

        value = landed[i, 0].astype(jnp.float32)
        for b in range(1, y_size):
            value += landed[i, b].astype(jnp.float32)
        out_ref[i] = value.astype(jnp.bfloat16)

    virt = {}

    def virt_start():
        virt["own"] = pltpu.make_async_copy(virt_ref, tile.at[x, c], own_sem)
        virt["own"].start()
        for name, side, to in (("p0", 0, xp), ("m1", 1, xm), ("p1", 1, xp), ("m0", 0, xm)):
            virt[name] = copies.go(virt_ref.at[sides[side]], tile.at[x, c, sides[side]], to)

    def virt_pass():
        for name, side, of, to in (("p", 0, x_down, xp), ("m", 1, x_up, xm)):
            virt[f"{name}{side}"].wait_recv()
            ref = tile.at[of, c, sides[side]]
            virt[name] = copies.go(ref, ref, to)
        virt["own over"] = copies.go(virt_ref, tile.at[x, c], sibling)

    def virt_over():
        virt["p1"].wait_recv()
        virt["m0"].wait_recv()
        for of, name in ((x_down, "down over"), (x_up, "up over")):
            virt[name] = copies.go(tile.at[of, c], tile.at[of, c], sibling)

    def virt_far():
        virt["p"].wait_recv()
        virt["m"].wait_recv()
        virt["far over"] = copies.go(tile.at[x_far, c], tile.at[x_far, c], sibling)

    def virt_end():
        virt["own"].wait()
        for name in ("own over", "down over", "up over", "far over"):
            virt[name].wait_recv()

    ready = 2 * far + 1
    events = [(0.5, virt_start), (3.5, virt_pass), (6.5, virt_over), (ready - 0.5, virt_far), (ready + 0.15, virt_end)]
    for k in chunks:
        at = STAGGER * k + 0.01 * k
        for t in range(far):
            events.append((at + t, functools.partial(scatter, t, k)))
            events.append((at + far + 1 + t, functools.partial(gather, t, k)))
        events.append((at + far, functools.partial(move, k)))
        events.append((at + ready, functools.partial(gathered, k)))
        for turn in range(x_size):
            events.append((at + ready + 0.2 + 0.5 * turn, functools.partial(product, k, turn)))
        events.append((at + ready + 4, functools.partial(finish, k)))
    for _, event in sorted(events, key=lambda one: one[0]):
        event()
    copies.wait_sends()
    for k in chunks:

        @pl.when(jnp.logical_not(itself[k]))
        def _(k=k):
            moving[k].wait_send()

    for remote, copy in leaving:
        if remote is None:
            copy.wait_send()
        else:

            @pl.when(remote)
            def _(copy=copy):
                copy.wait_send()


def body(three_center, block_pairs, occ_factor, virt_density, block_sizes, occ_mask, virt_mask):
    x_size, z_size = lax.axis_size("mu"), lax.axis_size("nu")
    y_size = x_size
    cores = lax.axis_size("ri") // y_size
    far = z_size // 2
    rows, occ_cols = occ_factor.shape
    p_rows, slots = three_center.shape[:2]
    width = virt_density.shape[1]
    blocks = block_sizes.shape[0] // x_size
    vmem = pl.BlockSpec(memory_space=pltpu.VMEM)
    dma = pltpu.SemaphoreType.DMA

    count = occ_copies(x_size, z_size) + 2 * far
    occ_all = pl.pallas_call(
        functools.partial(gather_occ, cores, x_size, z_size),
        out_shape=jax.ShapeDtypeStruct((x_size, z_size, rows, occ_cols), jnp.bfloat16),
        in_specs=[vmem],
        out_specs=vmem,
        scratch_shapes=[dma((count,)), dma((count,))],
        compiler_params=pltpu.CompilerParams(
            collective_id=0, has_side_effects=True, vmem_limit_bytes=16 * MIB
        ),
        name="gather_occ",
    )(occ_factor)

    group = SLOTS_A_STEP
    part, kept = pl.pallas_call(
        half_transform,
        grid_spec=pltpu.PrefetchScalarGridSpec(
            num_scalar_prefetch=4,
            grid=(slots // group,),
            in_specs=[
                pl.BlockSpec((p_rows, group, BS, BS), lambda g, *_: (0, g, 0, 0)),
                vmem,
                vmem,
            ],
            out_specs=[vmem, vmem],
            scratch_shapes=[pltpu.VMEM((p_rows, blocks, BS, occ_cols), jnp.float32)],
        ),
        out_shape=[
            jax.ShapeDtypeStruct((p_rows, blocks, BS, occ_cols), jnp.bfloat16),
            jax.ShapeDtypeStruct(virt_density.shape, jnp.bfloat16),
        ],
        compiler_params=pltpu.CompilerParams(vmem_limit_bytes=40 * MIB),
        name="half_transform",
    )(
        block_pairs, block_sizes, occ_mask, virt_mask,
        three_center, occ_all.reshape(x_size * z_size * rows // BS, BS, occ_cols), virt_density,
    )

    count = 16 * x_size + 16
    part = part.reshape(p_rows, z_size, rows, occ_cols)
    return pl.pallas_call(
        functools.partial(exchange, cores, x_size, z_size),
        out_shape=jax.ShapeDtypeStruct((p_rows, rows, occ_cols), jnp.bfloat16),
        in_specs=[vmem, vmem],
        out_specs=vmem,
        scratch_shapes=[
            pltpu.VMEM((x_size, cores, rows, width), jnp.bfloat16),
            pltpu.VMEM((2, x_size, far, rows, occ_cols), jnp.bfloat16),
            pltpu.VMEM((x_size, rows, occ_cols), jnp.bfloat16),
            pltpu.VMEM((x_size, z_size, rows, occ_cols), jnp.bfloat16),
            pltpu.VMEM((x_size, x_size, rows, occ_cols), jnp.bfloat16),
            pltpu.VMEM((p_rows, y_size, rows, occ_cols), jnp.bfloat16),
            dma((count,)),
            dma((count,)),
            dma((x_size,)),
            dma((x_size,)),
            dma((x_size * x_size,)),
            dma((p_rows * y_size,)),
            dma,
        ],
        compiler_params=pltpu.CompilerParams(
            collective_id=1, has_side_effects=True, vmem_limit_bytes=48 * MIB
        ),
        name="exchange",
    )(part, kept)


def solution(mesh):
    in_specs = (
        P("ri", ("mu", "nu"), None, None),
        P(("mu", "nu"), None),
        P(("mu", "nu"), None),
        P(("mu", "nu"), "ri"),
        P(),
        P(),
        P(),
    )
    out_specs = P("ri", ("mu", "nu"), None)
    return jax.shard_map(body, mesh=mesh, in_specs=in_specs, out_specs=out_specs, check_vma=False)
```

```python
import functools

import jax
import jax.numpy as jnp
from jax import lax
from jax.experimental import pallas as pl
from jax.experimental.pallas import tpu as pltpu
from jax.sharding import PartitionSpec as P

MESH = pl.DeviceIdType.MESH
BS = 128
STAGGER = 1
VIRT_TIMES = (0.3, 1.4, 5.4)
SLOTS_A_STEP = 8
MIB = 1 << 20


class Copies:
    def __init__(self, send, recv):
        self.send, self.recv, self.used = send, recv, 0
        self.started = []

    def make(self, src, dst, device):
        i = self.used
        self.used += 1
        return pltpu.make_async_remote_copy(
            src_ref=src,
            dst_ref=dst,
            send_sem=self.send.at[i],
            recv_sem=self.recv.at[i],
            device_id=device,
            device_id_type=MESH,
        )

    def go(self, src, dst, device):
        copy = self.make(src, dst, device)
        copy.start()
        self.started.append(copy)
        return copy

    def wait_sends(self):
        for copy in self.started:
            copy.wait_send()


def greet(devices):
    barrier = pltpu.get_barrier_semaphore()
    for device in devices:
        pl.semaphore_signal(barrier, inc=1, device_id=device, device_id_type=MESH)
    pl.semaphore_wait(barrier, len(devices))


def chain_slots(x_size, subs, pairs, prev, last, nu_of):
    slots, blocks = pairs.shape[0], last.shape[0] - 1
    first_block = lax.axis_index("mu") * blocks

    def clear(b, _):
        last[b] = slots
        return 0

    def link(k, _):
        mu = pairs[k, 0]
        block = jnp.where(mu >= 0, mu - first_block, blocks)
        prev[k] = last[block]
        last[block] = k
        nu = jnp.maximum(pairs[k, 1], 0)
        inner = lax.rem(nu, blocks)
        nu_of[k] = (lax.div(inner, subs) * x_size + lax.div(nu, blocks)) * subs + lax.rem(inner, subs)
        return 0

    lax.fori_loop(0, blocks + 1, clear, 0)
    lax.fori_loop(0, slots, link, 0)


def transform(
    cores, x_size, z_size,
    prev, last, nu_of, sizes, occ_mask, virt_mask,
    three_hbm, occ_ref, virt_ref, out_ref,
    occ_all, three, chain, part, kept, tile, sums, reduced, half, partial, landed,
    send, recv, plane_send, plane_recv, out_send, out_recv, own_sem, three_sem,
):
    x, z, r = lax.axis_index("mu"), lax.axis_index("nu"), lax.axis_index("ri")
    c, y = lax.rem(r, cores), r // cores
    y_size = x_size
    far = z_size // 2
    slots, occ_cols = prev.shape[0], occ_ref.shape[-1]
    subs = occ_ref.shape[0]
    rows = subs * BS
    zp, zm = {"nu": lax.rem(z + 1, z_size)}, {"nu": lax.rem(z + z_size - 1, z_size)}
    x_up, x_down = lax.rem(x + 1, x_size), lax.rem(x + x_size - 1, x_size)
    x_far = lax.rem(x + 2, x_size)
    xp, xm = {"mu": x_up}, {"mu": x_down}
    sibling = {"ri": r + 1 - 2 * c}
    ahead = lambda t: lax.rem(z + t + z_size, z_size)
    towards = (zp, zm)
    chunks = range(x_size)
    which = [lax.rem(k - y + y_size, y_size) for k in chunks]
    loads = [pltpu.make_async_copy(three_hbm.at[which[k]], three.at[k], three_sem.at[k]) for k in chunks]
    for load in loads:
        load.start()
    plane = [
        {"ri": lax.rem(y + b, y_size) * cores + c, "mu": lax.rem(x + a, x_size)}
        for b in range(y_size)
        for a in range(x_size)
        if a or b
    ]
    greet([zp, zm, sibling] + plane)
    copies = Copies(send, recv)
    bf16, f32 = jnp.bfloat16, jnp.float32

    span = BS // cores
    mine = pl.ds(pl.multiple_of(c * span, 16), span)
    lower = pl.ds(pl.multiple_of(c * span, 16), span // 2)
    upper = pl.ds(pl.multiple_of(c * span + span // 2, 16), span // 2)

    def here(column, shard, some):
        return occ_all.at[pl.ds((shard * x_size + column) * subs, subs), some]

    def across(shard):
        ref = occ_all.at[pl.ds(shard * x_size * subs, x_size * subs), mine]
        over.append(copies.go(ref, ref, sibling))

    over = []
    rising, falling = {}, {}

    def along_z(column, t):
        final = t == far - 1
        if t:
            rising[t - 1, column].wait_recv()
        ref = here(columns[column], ahead(-t), lower if final else mine)
        rising[t, column] = copies.go(ref, ref, zp)
        if t:
            falling[t - 1, column].wait_recv()
        ref = here(columns[column], ahead(t), upper if final else mine)
        falling[t, column] = copies.go(ref, ref, zm)

    columns = (x, x_down, x_up, x_far)
    own_block = (x * z_size + z) * subs
    occ_rows = lax.broadcasted_iota(jnp.int32, (span, occ_cols), 0) + c * span
    for b in range(subs):
        kept_rows = jnp.where(occ_mask[own_block + b] > 0, sizes[own_block + b], 0)
        occ_kept = jnp.where(occ_rows < kept_rows, occ_ref[b, mine, :].astype(f32), 0.0)
        occ_all[(z * x_size + x) * subs + b, mine, :] = occ_kept.astype(bf16)

    def mask_virt():
        row_ids = lax.broadcasted_iota(jnp.int32, (BS, BS), 0)
        col_ids = lax.broadcasted_iota(jnp.int32, (BS, BS), 1)
        col_blocks = virt_ref.shape[1] // BS
        for a in range(subs):
            for b in range(col_blocks):
                m_block = r * col_blocks + b
                kept_rows = jnp.where(virt_mask[own_block + a, m_block] > 0, sizes[own_block + a], 0)
                keep = (row_ids < kept_rows) & (col_ids < sizes[m_block])
                at = pl.ds(a * BS, BS), pl.ds(b * BS, BS)
                kept[at] = jnp.where(keep, virt_ref[at].astype(f32), 0.0).astype(bf16)

    virt = {}
    first, second = pl.ds(0, rows // 2), pl.ds(rows // 2, rows // 2)
    sides = (first, second)

    def virt_start():
        virt["own"] = pltpu.make_async_copy(kept, tile.at[x, c], own_sem)
        virt["own"].start()
        for name, side, to in (("p0", 0, xp), ("m1", 1, xm), ("p1", 1, xp), ("m0", 0, xm)):
            virt[name] = copies.go(kept.at[sides[side]], tile.at[x, c, sides[side]], to)

    def virt_pass():
        for name, side, of, to in (("p", 0, x_down, xp), ("m", 1, x_up, xm)):
            virt[f"{name}{side}"].wait_recv()
            ref = tile.at[of, c, sides[side]]
            virt[name] = copies.go(ref, ref, to)
        virt["own over"] = copies.go(kept, tile.at[x, c], sibling)

    def virt_over():
        virt["p1"].wait_recv()
        virt["m0"].wait_recv()
        for of, name in ((x_down, "down over"), (x_up, "up over")):
            virt[name] = copies.go(tile.at[of, c], tile.at[of, c], sibling)

    def virt_far():
        virt["p"].wait_recv()
        virt["m"].wait_recv()
        virt["far over"] = copies.go(tile.at[x_far, c], tile.at[x_far, c], sibling)

    def virt_end():
        virt["own"].wait()
        for name in ("own over", "down over", "up over", "far over"):
            virt[name].wait_recv()

    ref = here(x, z, mine)
    from_down, from_up = copies.go(ref, ref, xp), copies.go(ref, ref, xm)
    along_z(0, 0)
    mask_virt()
    chain[slots] = jnp.zeros(chain.shape[1:], f32)
    from_down.wait_recv()
    ref = here(x_down, z, lower)
    far_lower = copies.go(ref, ref, xp)
    from_up.wait_recv()
    ref = here(x_up, z, upper)
    far_upper = copies.go(ref, ref, xm)
    virt_start()
    along_z(1, 0)
    along_z(2, 0)
    far_lower.wait_recv()
    far_upper.wait_recv()
    along_z(3, 0)
    across(z)
    for t in range(1, far):
        for column in range(x_size):
            along_z(column, t)
        across(ahead(-t))
        across(ahead(t))
    for column in range(x_size):
        rising[far - 1, column].wait_recv()
        falling[far - 1, column].wait_recv()
    across(ahead(far))
    for copy in over:
        copy.wait_recv()

    itself = [(x == y) & (which[k] == x) for k in chunks]
    halves = (pl.ds(0, BS // 2), pl.ds(BS // 2, BS // 2))
    scattering, moving, gathering, leaving = {}, {}, {}, []

    def slot_sums(k):
        loads[k].wait()

        def some_slots(g, _):
            for j in range(SLOTS_A_STEP):
                slot = g * SLOTS_A_STEP + j
                product = jnp.dot(three[k, slot], occ_all[nu_of[slot]], preferred_element_type=f32)
                chain[slot] = product + chain[prev[slot]]
            return 0

        def one_shard(shard, _):
            for b in range(subs):
                part[k, shard, b] = chain[last[shard * subs + b]].astype(bf16)
            return 0

        lax.fori_loop(0, slots // SLOTS_A_STEP, some_slots, 0)
        lax.fori_loop(0, z_size, one_shard, 0)

    def scatter(t, k):
        for d in (0, 1):
            shard = ahead(far - t if d == 0 else t - far)
            a, b = halves[d], halves[1 - d]
            if t == 0:
                src = part.at[k, shard, :, a]
                dst = sums.at[d, k, 0, :, a]
            else:
                scattering[d, k, t - 1].wait_recv()
                src = sums.at[d, k, t - 1]
                dst = sums.at[d, k, t]
                if t == 1:
                    added = src[:, a, :].astype(f32) + part[k, shard, :, a, :].astype(f32)
                    src[:, a, :] = added.astype(bf16)
                    src[:, b, :] = part[k, shard, :, b, :]
                else:
                    added = src[...].astype(f32) + part[k, shard].astype(f32)
                    src[...] = added.astype(bf16)
            scattering[d, k, t] = copies.go(src, dst, towards[d])

    def move(k):
        for d in (0, 1):
            scattering[d, k, far - 1].wait_recv()
        added = part[k, z].astype(f32)
        added += sums[0, k, far - 1].astype(f32) + sums[1, k, far - 1].astype(f32)
        added = added.astype(bf16)
        copy = moving[k] = pltpu.make_async_remote_copy(
            src_ref=reduced.at[k],
            dst_ref=half.at[k, z],
            send_sem=plane_send.at[k],
            recv_sem=plane_recv.at[k],
            device_id={"ri": x * cores + c, "mu": which[k]},
            device_id_type=MESH,
        )

        @pl.when(itself[k])
        def _():
            half[k, z] = added

        @pl.when(jnp.logical_not(itself[k]))
        def _():
            reduced[k] = added
            copy.start()

    def gather(t, k):
        if t == 0:

            @pl.when(jnp.logical_not(itself[k]))
            def _():
                moving[k].wait_recv()

        for d in (0, 1):
            if t:
                gathering[d, k, t - 1].wait_recv()
            shard = ahead(-t if d == 0 else t)
            ref = half.at[k, shard, :, halves[d]] if t == far - 1 else half.at[k, shard]
            gathering[d, k, t] = copies.go(ref, ref, towards[d])

    def gathered(k):
        for d in (0, 1):
            gathering[d, k, far - 1].wait_recv()

    depth = z_size // cores

    def product(k, turn):
        off = (2, 1, 3, 0)[turn]
        column = lax.rem(x + off, x_size)
        value = None
        for b in range(cores):
            shards = half[k, b * depth : (b + 1) * depth].reshape(depth * rows, occ_cols)
            term = jnp.dot(tile[column, b], shards, preferred_element_type=f32)
            value = term if value is None else value + term
        value = value.astype(bf16)
        to_y = lax.rem(k - x + y_size, y_size)
        copy = pltpu.make_async_remote_copy(
            src_ref=partial.at[k, off],
            dst_ref=landed.at[x, y],
            send_sem=out_send.at[k * x_size + off],
            recv_sem=out_recv.at[x * y_size + y],
            device_id={"ri": to_y * cores + c, "mu": column},
            device_id_type=MESH,
        )
        if off:
            partial[k, off] = value
            copy.start()
            leaving.append((None, copy))
            return
        remote = to_y != y

        @pl.when(remote)
        def _():
            partial[k, off] = value
            copy.start()

        @pl.when(jnp.logical_not(remote))
        def _():
            landed[x, y] = value

        leaving.append((remote, copy))

    def finish(k):
        i = which[k]
        for b in range(y_size):
            arrival = pltpu.make_async_remote_copy(
                src_ref=partial.at[k, 0],
                dst_ref=landed.at[i, b],
                send_sem=out_send.at[k * x_size],
                recv_sem=out_recv.at[i * y_size + b],
                device_id=zp,
                device_id_type=MESH,
            )

            @pl.when(jnp.logical_not((i == x) & (y == b)))
            def _(arrival=arrival):
                arrival.wait_recv()

        value = landed[i, 0].astype(f32)
        for b in range(1, y_size):
            value += landed[i, b].astype(f32)
        out_ref[i] = value.astype(bf16)

    ready = 2 * far + 1
    events = [
        (VIRT_TIMES[0], virt_pass), (VIRT_TIMES[1], virt_over), (VIRT_TIMES[2], virt_far), (ready + 0.15, virt_end)
    ]
    for k in chunks:
        at = STAGGER * k + 0.01 * k
        events.append((at - 0.5, functools.partial(slot_sums, k)))
        for t in range(far):
            events.append((at + t, functools.partial(scatter, t, k)))
            events.append((at + far + 1 + t, functools.partial(gather, t, k)))
        events.append((at + far, functools.partial(move, k)))
        events.append((at + ready, functools.partial(gathered, k)))
        for turn in range(x_size):
            events.append((at + ready + 0.2 + 0.3 * turn, functools.partial(product, k, turn)))
        events.append((at + ready + 4, functools.partial(finish, k)))
    for _, event in sorted(events, key=lambda one: one[0]):
        event()
    copies.wait_sends()
    for k in chunks:

        @pl.when(jnp.logical_not(itself[k]))
        def _(k=k):
            moving[k].wait_send()

    for remote, copy in leaving:
        if remote is None:
            copy.wait_send()
        else:

            @pl.when(remote)
            def _(copy=copy):
                copy.wait_send()


def body(three_center, block_pairs, occ_factor, virt_density, block_sizes, occ_mask, virt_mask):
    x_size, z_size = lax.axis_size("mu"), lax.axis_size("nu")
    y_size = x_size
    cores = lax.axis_size("ri") // y_size
    far = z_size // 2
    rows, occ_cols = occ_factor.shape
    subs = rows // BS
    p_rows, slots = three_center.shape[:2]
    width = virt_density.shape[1]
    blocks = block_sizes.shape[0] // x_size
    vmem = pl.BlockSpec(memory_space=pltpu.VMEM)
    smem = pl.BlockSpec(memory_space=pltpu.SMEM)
    dma = pltpu.SemaphoreType.DMA
    bf16 = jnp.bfloat16

    prev, last, nu_of = pl.pallas_call(
        functools.partial(chain_slots, x_size, subs),
        out_shape=[jax.ShapeDtypeStruct((n,), jnp.int32) for n in (slots, blocks + 1, slots)],
        in_specs=[smem],
        out_specs=[smem] * 3,
        name="chain_slots",
    )(block_pairs)

    shard = (subs, BS, occ_cols)
    count = 6 * far * x_size + z_size + 14
    out = pl.pallas_call(
        functools.partial(transform, cores, x_size, z_size),
        out_shape=jax.ShapeDtypeStruct((p_rows, rows, occ_cols), bf16),
        in_specs=[smem] * 6 + [pl.BlockSpec(memory_space=pl.ANY), vmem, vmem],
        out_specs=vmem,
        scratch_shapes=[
            pltpu.VMEM((x_size * blocks, BS, occ_cols), bf16),
            pltpu.VMEM((p_rows, slots, BS, BS), bf16),
            pltpu.VMEM((slots + 1, BS, occ_cols), jnp.float32),
            pltpu.VMEM((p_rows, z_size) + shard, bf16),
            pltpu.VMEM((rows, width), bf16),
            pltpu.VMEM((x_size, cores, rows, width), bf16),
            pltpu.VMEM((2, x_size, far) + shard, bf16),
            pltpu.VMEM((x_size,) + shard, bf16),
            pltpu.VMEM((x_size, z_size) + shard, bf16),
            pltpu.VMEM((x_size, x_size, rows, occ_cols), bf16),
            pltpu.VMEM((p_rows, y_size, rows, occ_cols), bf16),
            dma((count,)),
            dma((count,)),
            dma((x_size,)),
            dma((x_size,)),
            dma((x_size * x_size,)),
            dma((p_rows * y_size,)),
            dma,
            dma((p_rows,)),
        ],
        compiler_params=pltpu.CompilerParams(
            collective_id=0, has_side_effects=True, vmem_limit_bytes=56 * MIB
        ),
        name="transform",
    )(
        prev, last, nu_of, block_sizes, occ_mask, virt_mask,
        three_center, occ_factor.reshape(shard), virt_density,
    )
    return out


def solution(mesh):
    in_specs = (
        P("ri", ("mu", "nu"), None, None),
        P(("mu", "nu"), None),
        P(("mu", "nu"), None),
        P(("mu", "nu"), "ri"),
        P(),
        P(),
        P(),
    )
    out_specs = P("ri", ("mu", "nu"), None)
    return jax.shard_map(body, mesh=mesh, in_specs=in_specs, out_specs=out_specs, check_vma=False)
```

```python
import functools

import jax
import jax.numpy as jnp
from jax import lax
from jax.experimental import pallas as pl
from jax.experimental.pallas import tpu as pltpu
from jax.sharding import PartitionSpec as P

MESH = pl.DeviceIdType.MESH
BS = 128
STARTS = (0, 0.5, 1.5, 2.5)
VIRT_TIMES = (2.4, 2.6, 6.4, 8.4)
SLOTS_A_STEP = 8
MIB = 1 << 20


class Copies:
    def __init__(self, send, recv):
        self.send, self.recv, self.used = send, recv, 0
        self.started = []

    def make(self, src, dst, device):
        i = self.used
        self.used += 1
        return pltpu.make_async_remote_copy(
            src_ref=src,
            dst_ref=dst,
            send_sem=self.send.at[i],
            recv_sem=self.recv.at[i],
            device_id=device,
            device_id_type=MESH,
        )

    def go(self, src, dst, device):
        copy = self.make(src, dst, device)
        copy.start()
        self.started.append(copy)
        return copy

    def wait_sends(self):
        for copy in self.started:
            copy.wait_send()


def greet(devices):
    barrier = pltpu.get_barrier_semaphore()
    for device in devices:
        pl.semaphore_signal(barrier, inc=1, device_id=device, device_id_type=MESH)
    pl.semaphore_wait(barrier, len(devices))


def chain_slots(blocks, x_size, subs, slots, pairs_ref, padded, rows_ref):
    lanes = padded.shape[1]
    padded[...] = jnp.full(padded.shape, -1, jnp.int32)
    padded[:, : pairs_ref.shape[1]] = pairs_ref[...]
    first_block = lax.axis_index("mu") * blocks
    mu = jnp.broadcast_to(padded[0:1, :] - first_block, (lanes, lanes))
    mu_down = mu.astype(jnp.float32).T.astype(jnp.int32)
    down = lax.broadcasted_iota(jnp.int32, (lanes, lanes), 0)
    along = lax.broadcasted_iota(jnp.int32, (lanes, lanes), 1)
    before = jnp.where((mu == mu_down) & (down < along), down, -1)
    prev = jnp.max(before, axis=0, keepdims=True)
    ends = jnp.max(jnp.where(mu_down == along, down, -1), axis=0, keepdims=True)
    nu = jnp.maximum(padded[1:2, :], 0)
    column, shard = jnp.zeros_like(nu), jnp.zeros_like(nu)
    for i in range(1, x_size):
        column += jnp.where(nu >= i * blocks, 1, 0)
    inner = nu - column * blocks
    for i in range(1, blocks // subs):
        shard += jnp.where(inner >= i * subs, 1, 0)
    sub = inner - shard * subs
    rows_ref[0:1, :] = jnp.where(prev < 0, slots, prev)
    rows_ref[1:2, :] = jnp.where(ends < 0, slots, ends)
    rows_ref[3:8, :] = jnp.zeros((5, lanes), jnp.int32)
    rows_ref[2:3, :] = (shard * x_size + column) * subs + sub


def transform(
    cores, x_size, z_size,
    sizes, occ_mask, virt_mask,
    pairs_ref, three_hbm, occ_ref, virt_ref, out_ref,
    occ_all, three, chain, part, kept, tile, total, summed, sums, reduced, half, partial, landed,
    send, recv, plane_send, plane_recv, out_send, out_recv, own_sem, three_sem,
    padded, plan_rows, plan, plan_sem,
):
    x, z, r = lax.axis_index("mu"), lax.axis_index("nu"), lax.axis_index("ri")
    c, y = lax.rem(r, cores), r // cores
    y_size = x_size
    far = z_size // 2
    slots, occ_cols = three_hbm.shape[1], occ_ref.shape[-1]
    subs = occ_ref.shape[0]
    rows = subs * BS
    zp, zm = {"nu": lax.rem(z + 1, z_size)}, {"nu": lax.rem(z + z_size - 1, z_size)}
    x_up, x_down = lax.rem(x + 1, x_size), lax.rem(x + x_size - 1, x_size)
    x_far = lax.rem(x + 2, x_size)
    xp, xm = {"mu": x_up}, {"mu": x_down}
    sibling = {"ri": r + 1 - 2 * c}
    ahead = lambda t: lax.rem(z + t + z_size, z_size)
    towards = (zp, zm)
    chunks = range(x_size)
    which = [lax.rem(k - y - x + 2 * y_size, y_size) for k in chunks]
    loads = [pltpu.make_async_copy(three_hbm.at[which[k]], three.at[k], three_sem.at[k]) for k in chunks]
    for load in loads:
        load.start()
    plane = [
        {"ri": lax.rem(y + b, y_size) * cores + c, "mu": lax.rem(x + a, x_size)}
        for b in range(y_size)
        for a in range(x_size)
        if a or b
    ]
    greet([zp, zm, sibling] + plane)
    copies = Copies(send, recv)
    bf16, f32 = jnp.bfloat16, jnp.float32

    span = BS // cores
    mine = pl.ds(pl.multiple_of(c * span, 16), span)
    lower = pl.ds(pl.multiple_of(c * span, 16), span // 2)
    upper = pl.ds(pl.multiple_of(c * span + span // 2, 16), span // 2)

    def here(column, shard, some):
        return occ_all.at[pl.ds((shard * x_size + column) * subs, subs), some]

    def across(shard):
        ref = occ_all.at[pl.ds(shard * x_size * subs, x_size * subs), mine]
        over.append(copies.go(ref, ref, sibling))

    over = []
    rising, falling = {}, {}

    def along_z(column, t):
        final = t == far - 1
        if t:
            rising[t - 1, column].wait_recv()
        ref = here(columns[column], ahead(-t), lower if final else mine)
        rising[t, column] = copies.go(ref, ref, zp)
        if t:
            falling[t - 1, column].wait_recv()
        ref = here(columns[column], ahead(t), upper if final else mine)
        falling[t, column] = copies.go(ref, ref, zm)

    columns = (x, x_down, x_up, x_far)
    own_block = (x * z_size + z) * subs
    occ_rows = lax.broadcasted_iota(jnp.int32, (span, occ_cols), 0) + c * span
    for b in range(subs):
        kept_rows = jnp.where(occ_mask[own_block + b] > 0, sizes[own_block + b], 0)
        occ_kept = jnp.where(occ_rows < kept_rows, occ_ref[b, mine, :].astype(f32), 0.0)
        occ_all[(z * x_size + x) * subs + b, mine, :] = occ_kept.astype(bf16)

    def mask_virt():
        row_ids = lax.broadcasted_iota(jnp.int32, (BS, BS), 0)
        col_ids = lax.broadcasted_iota(jnp.int32, (BS, BS), 1)
        col_blocks = virt_ref.shape[1] // BS
        for a in range(subs):
            for b in range(col_blocks):
                m_block = r * col_blocks + b
                kept_rows = jnp.where(virt_mask[own_block + a, m_block] > 0, sizes[own_block + a], 0)
                keep = (row_ids < kept_rows) & (col_ids < sizes[m_block])
                at = pl.ds(a * BS, BS), pl.ds(b * BS, BS)
                kept[at] = jnp.where(keep, virt_ref[at].astype(f32), 0.0).astype(bf16)

    virt = {}
    first, second = pl.ds(0, rows // 2), pl.ds(rows // 2, rows // 2)
    sides = (first, second)

    NEXT, FAR, BEFORE = 1, 2, 3

    def strip(distance, side=None):
        at, size = distance * rows, rows
        if side is not None:
            at, size = at + side * (rows // 2), rows // 2
        return tile.at[c, pl.ds(at, size)]

    def virt_start():
        virt["own"] = pltpu.make_async_copy(kept, strip(0), own_sem)
        virt["own"].start()
        for name, side, lands, to in (("p0", 0, BEFORE, xp), ("m1", 1, NEXT, xm), ("p1", 1, BEFORE, xp), ("m0", 0, NEXT, xm)):
            virt[name] = copies.go(kept.at[sides[side]], strip(lands, side), to)

    def virt_pass():
        for name, side, of, to in (("p", 0, BEFORE, xp), ("m", 1, NEXT, xm)):
            virt[f"{name}{side}"].wait_recv()
            virt[name] = copies.go(strip(of, side), strip(FAR, side), to)
        virt["own over"] = copies.go(kept, strip(0), sibling)

    def virt_over():
        virt["p1"].wait_recv()
        virt["m0"].wait_recv()
        for of, name in ((BEFORE, "down over"), (NEXT, "up over")):
            virt[name] = copies.go(strip(of), strip(of), sibling)

    def virt_far():
        virt["p"].wait_recv()
        virt["m"].wait_recv()
        virt["far over"] = copies.go(strip(FAR), strip(FAR), sibling)

    def virt_end():
        virt["own"].wait()
        for name in ("own over", "down over", "up over", "far over"):
            virt[name].wait_recv()

    ref = here(x, z, mine)
    from_down, from_up, from_far = [copies.go(ref, ref, to) for to in (xp, xm, {"mu": x_far})]
    along_z(0, 0)
    mask_virt()
    chain[slots] = jnp.zeros(chain.shape[1:], f32)
    chain_slots(z_size * subs, x_size, subs, slots, pairs_ref, padded, plan_rows)
    planning = pltpu.make_async_copy(plan_rows, plan, plan_sem)
    planning.start()
    from_down.wait_recv()
    along_z(1, 0)
    from_up.wait_recv()
    along_z(2, 0)
    from_far.wait_recv()
    along_z(3, 0)
    virt_start()
    across(z)
    for t in range(1, far):
        for column in range(x_size):
            along_z(column, t)
        across(ahead(-t))
        across(ahead(t))
    for column in range(x_size):
        rising[far - 1, column].wait_recv()
        falling[far - 1, column].wait_recv()
    across(ahead(far))
    for copy in over:
        copy.wait_recv()
    planning.wait()

    itself = [(x == y) & (which[k] == x) for k in chunks]
    halves = (pl.ds(0, BS // 2), pl.ds(BS // 2, BS // 2))
    scattering, moving, gathering, leaving = {}, {}, {}, []

    def slot_sums(k):
        loads[k].wait()

        def some_slots(g, _):
            for j in range(SLOTS_A_STEP):
                slot = g * SLOTS_A_STEP + j
                product = jnp.dot(three[k, slot], occ_all[plan[2, slot]], preferred_element_type=f32)
                chain[slot] = product + chain[plan[0, slot]]
            return 0

        def one_shard(shard, _):
            for b in range(subs):
                part[k, shard, b] = chain[plan[1, shard * subs + b]].astype(bf16)
            return 0

        lax.fori_loop(0, slots // SLOTS_A_STEP, some_slots, 0)
        lax.fori_loop(0, z_size, one_shard, 0)

    def scatter(t, k):
        for d in (0, 1):
            shard = ahead(far - t if d == 0 else t - far)
            a, b = halves[d], halves[1 - d]
            if t == 0:
                src = part.at[k, shard, :, a]
                dst = sums.at[d, k, 0, :, a]
            else:
                scattering[d, k, t - 1].wait_recv()
                src = sums.at[d, k, t - 1]
                dst = sums.at[d, k, t]
                if t == 1:
                    added = src[:, a, :].astype(f32) + part[k, shard, :, a, :].astype(f32)
                    src[:, a, :] = added.astype(bf16)
                    src[:, b, :] = part[k, shard, :, b, :]
                else:
                    added = src[...].astype(f32) + part[k, shard].astype(f32)
                    src[...] = added.astype(bf16)
            scattering[d, k, t] = copies.go(src, dst, towards[d])

    def move(k):
        for d in (0, 1):
            scattering[d, k, far - 1].wait_recv()
        added = part[k, z].astype(f32)
        added += sums[0, k, far - 1].astype(f32) + sums[1, k, far - 1].astype(f32)
        added = added.astype(bf16)
        copy = moving[k] = pltpu.make_async_remote_copy(
            src_ref=reduced.at[k],
            dst_ref=half.at[k, z],
            send_sem=plane_send.at[k],
            recv_sem=plane_recv.at[k],
            device_id={"ri": x * cores + c, "mu": which[k]},
            device_id_type=MESH,
        )

        @pl.when(itself[k])
        def _():
            half[k, z] = added

        @pl.when(jnp.logical_not(itself[k]))
        def _():
            reduced[k] = added
            copy.start()

    def gather(t, k):
        if t == 0:

            @pl.when(jnp.logical_not(itself[k]))
            def _():
                moving[k].wait_recv()

        for d in (0, 1):
            if t:
                gathering[d, k, t - 1].wait_recv()
            shard = ahead(-t if d == 0 else t)
            ref = half.at[k, shard, :, halves[d]] if t == far - 1 else half.at[k, shard]
            gathering[d, k, t] = copies.go(ref, ref, towards[d])

    def gathered(k):
        for d in (0, 1):
            gathering[d, k, far - 1].wait_recv()

    depth = z_size // cores

    def shard_term(k, distance, at=0, size=x_size * rows):
        shard = ahead(distance)
        cols = pl.ds(pl.multiple_of(lax.rem(shard, depth) * rows, BS), rows)
        return jnp.dot(
            tile[shard // depth, at : at + size, cols],
            half[k, shard].reshape(rows, occ_cols),
            preferred_element_type=f32,
        )

    def grow(k, distances):
        for distance in distances:
            term = shard_term(k, distance)
            total[...] = term if distance == 0 else total[...] + term

    def whole(k):
        value = None
        for b in range(cores):
            shards = half[k, b * depth : (b + 1) * depth].reshape(depth * rows, occ_cols)
            term = jnp.dot(tile[b], shards, preferred_element_type=f32)
            value = term if value is None else value + term
        total[...] = value

    def product(k, turn):
        off = (FAR, NEXT, BEFORE, 0)[turn]
        column = lax.rem(x + off, x_size)
        value = total[off * rows : (off + 1) * rows]
        if k == x_size - 1:
            value = value + shard_term(k, far, off * rows, rows)
        value = value.astype(bf16)
        to_y = which[k]
        copy = pltpu.make_async_remote_copy(
            src_ref=partial.at[k, off],
            dst_ref=landed.at[x, y],
            send_sem=out_send.at[k * x_size + off],
            recv_sem=out_recv.at[x * y_size + y],
            device_id={"ri": to_y * cores + c, "mu": column},
            device_id_type=MESH,
        )
        if off:
            partial[k, off] = value
            copy.start()
            leaving.append((None, copy))
            return
        remote = to_y != y

        @pl.when(remote)
        def _():
            partial[k, off] = value
            copy.start()

        @pl.when(jnp.logical_not(remote))
        def _():
            landed[x, y] = value

        leaving.append((remote, copy))

    def finish(k):
        for b in range(y_size):
            i = lax.rem(k - y - b + 2 * y_size, y_size)
            arrival = pltpu.make_async_remote_copy(
                src_ref=partial.at[k, 0],
                dst_ref=landed.at[i, b],
                send_sem=out_send.at[k * x_size],
                recv_sem=out_recv.at[i * y_size + b],
                device_id=zp,
                device_id_type=MESH,
            )

            @pl.when(jnp.logical_not((i == x) & (y == b)))
            def _(arrival=arrival):
                arrival.wait_recv()

            value = landed[i, b].astype(f32)
            if k:
                value = value + summed[i]
            if k < x_size - 1:
                summed[i] = value
            else:
                out_ref[i] = value.astype(bf16)

    ready = 2 * far + 1
    events = [
        (VIRT_TIMES[0], virt_pass), (VIRT_TIMES[1], virt_over), (VIRT_TIMES[2], virt_far), (VIRT_TIMES[3], virt_end)
    ]
    for k in chunks:
        at = STARTS[k] + 0.01 * k
        events.append((at - 0.5, functools.partial(slot_sums, k)))
        for t in range(far):
            events.append((at + t, functools.partial(scatter, t, k)))
            events.append((at + far + 1 + t, functools.partial(gather, t, k)))
            if k == x_size - 1:
                events.append((max(at + far + 1 + t, STARTS[k - 1] + ready + 0.3) + 0.05, functools.partial(grow, k, (-t, t) if t else (0,))))
        events.append((at + far, functools.partial(move, k)))
        events.append((at + ready, functools.partial(gathered, k)))
        if k < x_size - 1:
            events.append((at + ready + 0.1, functools.partial(whole, k)))
        for turn in range(x_size):
            events.append((at + ready + 0.2 + 0.01 * turn, functools.partial(product, k, turn)))
        events.append((at + ready + 3, functools.partial(finish, k)))
    for _, event in sorted(events, key=lambda one: one[0]):
        event()
    copies.wait_sends()
    for k in chunks:

        @pl.when(jnp.logical_not(itself[k]))
        def _(k=k):
            moving[k].wait_send()

    for remote, copy in leaving:
        if remote is None:
            copy.wait_send()
        else:

            @pl.when(remote)
            def _(copy=copy):
                copy.wait_send()


def body(three_center, block_pairs, occ_factor, virt_density, block_sizes, occ_mask, virt_mask):
    x_size, z_size = lax.axis_size("mu"), lax.axis_size("nu")
    y_size = x_size
    cores = lax.axis_size("ri") // y_size
    far = z_size // 2
    rows, occ_cols = occ_factor.shape
    subs = rows // BS
    p_rows, slots = three_center.shape[:2]
    width = virt_density.shape[1]
    blocks = block_sizes.shape[0] // x_size
    vmem = pl.BlockSpec(memory_space=pltpu.VMEM)
    smem = pl.BlockSpec(memory_space=pltpu.SMEM)
    dma = pltpu.SemaphoreType.DMA
    bf16 = jnp.bfloat16

    shard = (subs, BS, occ_cols)
    count = 6 * far * x_size + z_size + 14
    out = pl.pallas_call(
        functools.partial(transform, cores, x_size, z_size),
        out_shape=jax.ShapeDtypeStruct((p_rows, rows, occ_cols), bf16),
        in_specs=[smem] * 3 + [vmem, pl.BlockSpec(memory_space=pl.ANY), vmem, vmem],
        out_specs=vmem,
        scratch_shapes=[
            pltpu.VMEM((x_size * blocks, BS, occ_cols), bf16),
            pltpu.VMEM((p_rows, slots, BS, BS), bf16),
            pltpu.VMEM((slots + 1, BS, occ_cols), jnp.float32),
            pltpu.VMEM((p_rows, z_size) + shard, bf16),
            pltpu.VMEM((rows, width), bf16),
            pltpu.VMEM((cores, x_size * rows, width), bf16),
            pltpu.VMEM((x_size * rows, occ_cols), jnp.float32),
            pltpu.VMEM((p_rows, rows, occ_cols), jnp.float32),
            pltpu.VMEM((2, x_size, far) + shard, bf16),
            pltpu.VMEM((x_size,) + shard, bf16),
            pltpu.VMEM((x_size, z_size) + shard, bf16),
            pltpu.VMEM((x_size, x_size, rows, occ_cols), bf16),
            pltpu.VMEM((p_rows, y_size, rows, occ_cols), bf16),
            dma((count,)),
            dma((count,)),
            dma((x_size,)),
            dma((x_size,)),
            dma((x_size * x_size,)),
            dma((p_rows * y_size,)),
            dma,
            dma((p_rows,)),
            pltpu.VMEM((2, BS), jnp.int32),
            pltpu.VMEM((8, BS), jnp.int32),
            pltpu.SMEM((8, BS), jnp.int32),
            dma,
        ],
        compiler_params=pltpu.CompilerParams(
            collective_id=0, has_side_effects=True, vmem_limit_bytes=56 * MIB
        ),
        name="transform",
    )(
        block_sizes, occ_mask, virt_mask,
        block_pairs.T, three_center, occ_factor.reshape(shard), virt_density,
    )
    return out


def solution(mesh):
    in_specs = (
        P("ri", ("mu", "nu"), None, None),
        P(("mu", "nu"), None),
        P(("mu", "nu"), None),
        P(("mu", "nu"), "ri"),
        P(),
        P(),
        P(),
    )
    out_specs = P("ri", ("mu", "nu"), None)
    return jax.shard_map(body, mesh=mesh, in_specs=in_specs, out_specs=out_specs, check_vma=False)
```

```python
import functools

import jax
import jax.numpy as jnp
from jax import lax
from jax.experimental import pallas as pl
from jax.experimental.pallas import tpu as pltpu
from jax.sharding import PartitionSpec as P

MESH = pl.DeviceIdType.MESH
BS = 128
STARTS = (0, 0.5, 1.5, 2.5)
VIRT_TIMES = (2.4, 2.6, 6.4, 8.4)
SLOTS_A_STEP = 18
MIB = 1 << 20


class Copies:
    def __init__(self, send, recv):
        self.send, self.recv, self.used = send, recv, 0
        self.started = []

    def make(self, src, dst, device):
        i = self.used
        self.used += 1
        return pltpu.make_async_remote_copy(
            src_ref=src,
            dst_ref=dst,
            send_sem=self.send.at[i],
            recv_sem=self.recv.at[i],
            device_id=device,
            device_id_type=MESH,
        )

    def go(self, src, dst, device):
        copy = self.make(src, dst, device)
        copy.start()
        self.started.append(copy)
        return copy

    def wait_sends(self):
        for copy in self.started:
            copy.wait_send()


def greet(devices):
    barrier = pltpu.get_barrier_semaphore()
    for device in devices:
        pl.semaphore_signal(barrier, inc=1, device_id=device, device_id_type=MESH)
    pl.semaphore_wait(barrier, len(devices))


def chain_slots(blocks, x_size, subs, slots, pairs_ref, padded, rows_ref):
    lanes = padded.shape[1]
    padded[...] = jnp.full(padded.shape, -1, jnp.int32)
    padded[:, : pairs_ref.shape[1]] = pairs_ref[...]
    first_block = lax.axis_index("mu") * blocks
    mu = jnp.broadcast_to(padded[0:1, :] - first_block, (lanes, lanes))
    mu_down = mu.astype(jnp.float32).T.astype(jnp.int32)
    down = lax.broadcasted_iota(jnp.int32, (lanes, lanes), 0)
    along = lax.broadcasted_iota(jnp.int32, (lanes, lanes), 1)
    before = jnp.where((mu == mu_down) & (down < along), down, -1)
    prev = jnp.max(before, axis=0, keepdims=True)
    ends = jnp.max(jnp.where(mu_down == along, down, -1), axis=0, keepdims=True)
    nu = jnp.maximum(padded[1:2, :], 0)
    column, shard = jnp.zeros_like(nu), jnp.zeros_like(nu)
    for i in range(1, x_size):
        column += jnp.where(nu >= i * blocks, 1, 0)
    inner = nu - column * blocks
    for i in range(1, blocks // subs):
        shard += jnp.where(inner >= i * subs, 1, 0)
    sub = inner - shard * subs
    rows_ref[0:1, :] = jnp.where(prev < 0, slots, prev)
    rows_ref[1:2, :] = jnp.where(ends < 0, slots, ends)
    rows_ref[3:8, :] = jnp.zeros((5, lanes), jnp.int32)
    rows_ref[2:3, :] = (shard * x_size + column) * subs + sub


def transform(
    cores, x_size, z_size,
    sizes, occ_mask, virt_mask,
    pairs_ref, three_hbm, occ_ref, virt_ref, out_ref,
    occ_all, three, chain, part, kept, tile, total, summed, sums, reduced, half, partial, landed,
    send, recv, plane_send, plane_recv, out_send, out_recv, own_sem, three_sem,
    padded, plan_rows, plan, plan_sem,
):
    x, z, r = lax.axis_index("mu"), lax.axis_index("nu"), lax.axis_index("ri")
    c, y = lax.rem(r, cores), r // cores
    y_size = x_size
    far = z_size // 2
    slots, occ_cols = three_hbm.shape[1], occ_ref.shape[-1]
    subs = occ_ref.shape[0]
    rows = subs * BS
    zp, zm = {"nu": lax.rem(z + 1, z_size)}, {"nu": lax.rem(z + z_size - 1, z_size)}
    x_up, x_down = lax.rem(x + 1, x_size), lax.rem(x + x_size - 1, x_size)
    x_far = lax.rem(x + 2, x_size)
    xp, xm = {"mu": x_up}, {"mu": x_down}
    sibling = {"ri": r + 1 - 2 * c}
    ahead = lambda t: lax.rem(z + t + z_size, z_size)
    towards = (zp, zm)
    chunks = range(x_size)
    which = [lax.rem(k - y - x + 2 * y_size, y_size) for k in chunks]
    loads = [pltpu.make_async_copy(three_hbm.at[which[k]], three.at[k], three_sem.at[k]) for k in chunks]
    for load in loads:
        load.start()
    plane = [
        {"ri": lax.rem(y + b, y_size) * cores + c, "mu": lax.rem(x + a, x_size)}
        for b in range(y_size)
        for a in range(x_size)
        if a or b
    ]
    greet([zp, zm, sibling] + plane)
    copies = Copies(send, recv)
    bf16, f32 = jnp.bfloat16, jnp.float32

    span = BS // cores
    mine = pl.ds(pl.multiple_of(c * span, 16), span)
    lower = pl.ds(pl.multiple_of(c * span, 16), span // 2)
    upper = pl.ds(pl.multiple_of(c * span + span // 2, 16), span // 2)

    def here(column, shard, some):
        return occ_all.at[pl.ds((shard * x_size + column) * subs, subs), some]

    def across(shard):
        ref = occ_all.at[pl.ds(shard * x_size * subs, x_size * subs), mine]
        over.append(copies.go(ref, ref, sibling))

    over = []
    rising, falling = {}, {}

    def along_z(column, t):
        final = t == far - 1
        if t:
            rising[t - 1, column].wait_recv()
        ref = here(columns[column], ahead(-t), lower if final else mine)
        rising[t, column] = copies.go(ref, ref, zp)
        if t:
            falling[t - 1, column].wait_recv()
        ref = here(columns[column], ahead(t), upper if final else mine)
        falling[t, column] = copies.go(ref, ref, zm)

    columns = (x, x_down, x_up, x_far)
    own_block = (x * z_size + z) * subs
    occ_rows = lax.broadcasted_iota(jnp.int32, (span, occ_cols), 0) + c * span
    for b in range(subs):
        kept_rows = jnp.where(occ_mask[own_block + b] > 0, sizes[own_block + b], 0)
        occ_kept = jnp.where(occ_rows < kept_rows, occ_ref[b, mine, :].astype(f32), 0.0)
        occ_all[(z * x_size + x) * subs + b, mine, :] = occ_kept.astype(bf16)

    def mask_virt():
        row_ids = lax.broadcasted_iota(jnp.int32, (BS, BS), 0)
        col_ids = lax.broadcasted_iota(jnp.int32, (BS, BS), 1)
        col_blocks = virt_ref.shape[1] // BS
        for a in range(subs):
            for b in range(col_blocks):
                m_block = r * col_blocks + b
                kept_rows = jnp.where(virt_mask[own_block + a, m_block] > 0, sizes[own_block + a], 0)
                keep = (row_ids < kept_rows) & (col_ids < sizes[m_block])
                at = pl.ds(a * BS, BS), pl.ds(b * BS, BS)
                kept[at] = jnp.where(keep, virt_ref[at].astype(f32), 0.0).astype(bf16)

    virt = {}
    first, second = pl.ds(0, rows // 2), pl.ds(rows // 2, rows // 2)
    sides = (first, second)

    NEXT, FAR, BEFORE = 1, 2, 3

    def strip(distance, side=None):
        at, size = distance * rows, rows
        if side is not None:
            at, size = at + side * (rows // 2), rows // 2
        return tile.at[c, pl.ds(at, size)]

    def virt_start():
        virt["own"] = pltpu.make_async_copy(kept, strip(0), own_sem)
        virt["own"].start()
        for name, side, lands, to in (("p0", 0, BEFORE, xp), ("m1", 1, NEXT, xm), ("p1", 1, BEFORE, xp), ("m0", 0, NEXT, xm)):
            virt[name] = copies.go(kept.at[sides[side]], strip(lands, side), to)

    def virt_pass():
        for name, side, of, to in (("p", 0, BEFORE, xp), ("m", 1, NEXT, xm)):
            virt[f"{name}{side}"].wait_recv()
            virt[name] = copies.go(strip(of, side), strip(FAR, side), to)
        virt["own over"] = copies.go(kept, strip(0), sibling)

    def virt_over():
        virt["p1"].wait_recv()
        virt["m0"].wait_recv()
        for of, name in ((BEFORE, "down over"), (NEXT, "up over")):
            virt[name] = copies.go(strip(of), strip(of), sibling)

    def virt_far():
        virt["p"].wait_recv()
        virt["m"].wait_recv()
        virt["far over"] = copies.go(strip(FAR), strip(FAR), sibling)

    def virt_end():
        virt["own"].wait()
        for name in ("own over", "down over", "up over", "far over"):
            virt[name].wait_recv()

    ref = here(x, z, mine)
    from_down, from_up, from_far = [copies.go(ref, ref, to) for to in (xp, xm, {"mu": x_far})]
    along_z(0, 0)
    mask_virt()
    chain[slots] = jnp.zeros(chain.shape[1:], f32)
    chain_slots(z_size * subs, x_size, subs, slots, pairs_ref, padded, plan_rows)
    planning = pltpu.make_async_copy(plan_rows, plan, plan_sem)
    planning.start()
    from_down.wait_recv()
    along_z(1, 0)
    from_up.wait_recv()
    along_z(2, 0)
    from_far.wait_recv()
    along_z(3, 0)
    virt_start()
    across(z)
    for t in range(1, far):
        for column in range(x_size):
            along_z(column, t)
        across(ahead(-t))
        across(ahead(t))
    for column in range(x_size):
        rising[far - 1, column].wait_recv()
        falling[far - 1, column].wait_recv()
    across(ahead(far))
    for copy in over:
        copy.wait_recv()
    planning.wait()

    itself = [(x == y) & (which[k] == x) for k in chunks]
    halves = (pl.ds(0, BS // 2), pl.ds(BS // 2, BS // 2))
    scattering, moving, gathering, leaving = {}, {}, {}, []

    def slot_sums(k):
        loads[k].wait()

        def some_slots(g, _):
            for j in range(SLOTS_A_STEP):
                slot = g * SLOTS_A_STEP + j
                product = jnp.dot(three[k, slot], occ_all[plan[2, slot]], preferred_element_type=f32)
                chain[slot] = product + chain[plan[0, slot]]
            return 0

        def one_shard(shard, _):
            for b in range(subs):
                part[k, shard, b] = chain[plan[1, shard * subs + b]].astype(bf16)
            return 0

        lax.fori_loop(0, slots // SLOTS_A_STEP, some_slots, 0)
        lax.fori_loop(0, z_size, one_shard, 0)

    def scatter(t, k):
        for d in (0, 1):
            shard = ahead(far - t if d == 0 else t - far)
            a, b = halves[d], halves[1 - d]
            if t == 0:
                src = part.at[k, shard, :, a]
                dst = sums.at[d, k, 0, :, a]
            else:
                scattering[d, k, t - 1].wait_recv()
                src = sums.at[d, k, t - 1]
                dst = sums.at[d, k, t]
                if t == 1:
                    added = src[:, a, :].astype(f32) + part[k, shard, :, a, :].astype(f32)
                    src[:, a, :] = added.astype(bf16)
                    src[:, b, :] = part[k, shard, :, b, :]
                else:
                    added = src[...].astype(f32) + part[k, shard].astype(f32)
                    src[...] = added.astype(bf16)
            scattering[d, k, t] = copies.go(src, dst, towards[d])

    def move(k):
        for d in (0, 1):
            scattering[d, k, far - 1].wait_recv()
        added = part[k, z].astype(f32)
        added += sums[0, k, far - 1].astype(f32) + sums[1, k, far - 1].astype(f32)
        added = added.astype(bf16)
        copy = moving[k] = pltpu.make_async_remote_copy(
            src_ref=reduced.at[k],
            dst_ref=half.at[k, z],
            send_sem=plane_send.at[k],
            recv_sem=plane_recv.at[k],
            device_id={"ri": x * cores + c, "mu": which[k]},
            device_id_type=MESH,
        )

        @pl.when(itself[k])
        def _():
            half[k, z] = added

        @pl.when(jnp.logical_not(itself[k]))
        def _():
            reduced[k] = added
            copy.start()

    def gather(t, k):
        if t == 0:

            @pl.when(jnp.logical_not(itself[k]))
            def _():
                moving[k].wait_recv()

        for d in (0, 1):
            if t:
                gathering[d, k, t - 1].wait_recv()
            shard = ahead(-t if d == 0 else t)
            ref = half.at[k, shard, :, halves[d]] if t == far - 1 else half.at[k, shard]
            gathering[d, k, t] = copies.go(ref, ref, towards[d])

    def gathered(k):
        for d in (0, 1):
            gathering[d, k, far - 1].wait_recv()

    depth = z_size // cores

    def shard_term(k, distance, at=0, size=x_size * rows):
        shard = ahead(distance)
        cols = pl.ds(pl.multiple_of(lax.rem(shard, depth) * rows, BS), rows)
        return jnp.dot(
            tile[shard // depth, at : at + size, cols],
            half[k, shard].reshape(rows, occ_cols),
            preferred_element_type=f32,
        )

    def grow(k, distances):
        for distance in distances:
            term = shard_term(k, distance)
            total[...] = term if distance == 0 else total[...] + term

    def whole(k):
        value = None
        for b in range(cores):
            shards = half[k, b * depth : (b + 1) * depth].reshape(depth * rows, occ_cols)
            term = jnp.dot(tile[b], shards, preferred_element_type=f32)
            value = term if value is None else value + term
        total[...] = value

    def product(k, turn):
        off = (FAR, NEXT, BEFORE, 0)[turn]
        column = lax.rem(x + off, x_size)
        value = total[off * rows : (off + 1) * rows]
        if k == x_size - 1:
            value = value + shard_term(k, far, off * rows, rows)
        value = value.astype(bf16)
        to_y = which[k]
        copy = pltpu.make_async_remote_copy(
            src_ref=partial.at[k, off],
            dst_ref=landed.at[x, y],
            send_sem=out_send.at[k * x_size + off],
            recv_sem=out_recv.at[x * y_size + y],
            device_id={"ri": to_y * cores + c, "mu": column},
            device_id_type=MESH,
        )
        if off:
            partial[k, off] = value
            copy.start()
            leaving.append((None, copy))
            return
        remote = to_y != y

        @pl.when(remote)
        def _():
            partial[k, off] = value
            copy.start()

        @pl.when(jnp.logical_not(remote))
        def _():
            landed[x, y] = value

        leaving.append((remote, copy))

    def finish(k):
        for b in range(y_size):
            i = lax.rem(k - y - b + 2 * y_size, y_size)
            arrival = pltpu.make_async_remote_copy(
                src_ref=partial.at[k, 0],
                dst_ref=landed.at[i, b],
                send_sem=out_send.at[k * x_size],
                recv_sem=out_recv.at[i * y_size + b],
                device_id=zp,
                device_id_type=MESH,
            )

            @pl.when(jnp.logical_not((i == x) & (y == b)))
            def _(arrival=arrival):
                arrival.wait_recv()

            value = landed[i, b].astype(f32)
            if k:
                value = value + summed[i]
            if k < x_size - 1:
                summed[i] = value
            else:
                out_ref[i] = value.astype(bf16)

    def sent():
        copies.wait_sends()
        for k in chunks:

            @pl.when(jnp.logical_not(itself[k]))
            def _(k=k):
                moving[k].wait_send()

        for remote, copy in leaving:
            if remote is None:
                copy.wait_send()
            else:

                @pl.when(remote)
                def _(copy=copy):
                    copy.wait_send()

    ready = 2 * far + 1
    events = [
        (VIRT_TIMES[0], virt_pass), (VIRT_TIMES[1], virt_over), (VIRT_TIMES[2], virt_far), (VIRT_TIMES[3], virt_end)
    ]
    for k in chunks:
        at = STARTS[k] + 0.01 * k
        events.append((at - 0.5, functools.partial(slot_sums, k)))
        for t in range(far):
            events.append((at + t, functools.partial(scatter, t, k)))
            events.append((at + far + 1 + t, functools.partial(gather, t, k)))
            if k == x_size - 1:
                events.append((max(at + far + 1 + t, STARTS[k - 1] + ready + 0.3) + 0.05, functools.partial(grow, k, (-t, t) if t else (0,))))
        events.append((at + far, functools.partial(move, k)))
        events.append((at + ready, functools.partial(gathered, k)))
        if k < x_size - 1:
            events.append((at + ready + 0.1, functools.partial(whole, k)))
        for turn in range(x_size):
            events.append((at + ready + 0.2 + 0.01 * turn, functools.partial(product, k, turn)))
        events.append((at + ready + 3, functools.partial(finish, k)))
    events.append((STARTS[-1] + ready + 2.9, sent))
    for _, event in sorted(events, key=lambda one: one[0]):
        event()


def body(three_center, block_pairs, occ_factor, virt_density, block_sizes, occ_mask, virt_mask):
    x_size, z_size = lax.axis_size("mu"), lax.axis_size("nu")
    y_size = x_size
    cores = lax.axis_size("ri") // y_size
    far = z_size // 2
    rows, occ_cols = occ_factor.shape
    subs = rows // BS
    p_rows, slots = three_center.shape[:2]
    width = virt_density.shape[1]
    blocks = block_sizes.shape[0] // x_size
    vmem = pl.BlockSpec(memory_space=pltpu.VMEM)
    smem = pl.BlockSpec(memory_space=pltpu.SMEM)
    dma = pltpu.SemaphoreType.DMA
    bf16 = jnp.bfloat16

    shard = (subs, BS, occ_cols)
    count = 6 * far * x_size + z_size + 14
    out = pl.pallas_call(
        functools.partial(transform, cores, x_size, z_size),
        out_shape=jax.ShapeDtypeStruct((p_rows, rows, occ_cols), bf16),
        in_specs=[smem] * 3 + [vmem, pl.BlockSpec(memory_space=pl.ANY), vmem, vmem],
        out_specs=vmem,
        scratch_shapes=[
            pltpu.VMEM((x_size * blocks, BS, occ_cols), bf16),
            pltpu.VMEM((p_rows, slots, BS, BS), bf16),
            pltpu.VMEM((slots + 1, BS, occ_cols), jnp.float32),
            pltpu.VMEM((p_rows, z_size) + shard, bf16),
            pltpu.VMEM((rows, width), bf16),
            pltpu.VMEM((cores, x_size * rows, width), bf16),
            pltpu.VMEM((x_size * rows, occ_cols), jnp.float32),
            pltpu.VMEM((p_rows, rows, occ_cols), jnp.float32),
            pltpu.VMEM((2, x_size, far) + shard, bf16),
            pltpu.VMEM((x_size,) + shard, bf16),
            pltpu.VMEM((x_size, z_size) + shard, bf16),
            pltpu.VMEM((x_size, x_size, rows, occ_cols), bf16),
            pltpu.VMEM((p_rows, y_size, rows, occ_cols), bf16),
            dma((count,)),
            dma((count,)),
            dma((x_size,)),
            dma((x_size,)),
            dma((x_size * x_size,)),
            dma((p_rows * y_size,)),
            dma,
            dma((p_rows,)),
            pltpu.VMEM((2, BS), jnp.int32),
            pltpu.VMEM((8, BS), jnp.int32),
            pltpu.SMEM((8, BS), jnp.int32),
            dma,
        ],
        compiler_params=pltpu.CompilerParams(
            collective_id=0, has_side_effects=True, vmem_limit_bytes=56 * MIB
        ),
        name="transform",
    )(
        block_sizes, occ_mask, virt_mask,
        block_pairs.T, three_center, occ_factor.reshape(shard), virt_density,
    )
    return out


def solution(mesh):
    in_specs = (
        P("ri", ("mu", "nu"), None, None),
        P(("mu", "nu"), None),
        P(("mu", "nu"), None),
        P(("mu", "nu"), "ri"),
        P(),
        P(),
        P(),
    )
    out_specs = P("ri", ("mu", "nu"), None)
    return jax.shard_map(body, mesh=mesh, in_specs=in_specs, out_specs=out_specs, check_vma=False)
```
